256 devices in a mesh: seq: 32 (over z_lo, x, core), tp: 8 (over z_hi, y).
Axes of the slice: x: 4, y: 4, z: 8 (z_hi: 2, z_lo: 4; z = z_hi * 4 + z_lo), core: 2. Of those that a mesh axis runs over, the one named last changes fastest.
Arguments:
- tokens: bfloat16 [2048, 8192], P('seq', 'tp'), may hold values from -6 to 6
- out_grad: bfloat16 [2048, 8192], P('seq', 'tp'), may hold values from -6 to 6
- w_in: bfloat16 [8192, 16384], P('tp', 'seq'), may hold values from -0.0625 to 0.0625
- w_out: bfloat16 [16384, 8192], P('seq', 'tp'), may hold values from -0.046875 to 0.046875
- sketch: bfloat16 [2048, 256], P('seq'), may hold values from -0.375 to 0.375
Outputs:
- input_grad: bfloat16 [2048, 8192], P('seq', 'tp')
- grad_in: bfloat16 [8192, 16384], P('tp', 'seq')
- grad_out: bfloat16 [16384, 8192], P('seq', 'tp')
The draws below stay inside these ranges and needn't reach their ends.
All inputs are finite; a program needn't handle non-finite values.
Results may differ from the reference program's by a relative error of at most 0.0063.
Values may be sent and summed in bfloat16 or wider, within the bound.
A program may use at most 128 MiB of HBM per device.

```python
import math
import jax
import jax.numpy as jnp
from jax import lax

D = 8192
FF = 16384
SKETCH = 256
TOKENS = 2048


def shard_levels(rng, shape, shards, low, largest):
    def one(axis_at, blocks):
        draws = jax.random.uniform(jax.random.fold_in(jax.random.fold_in(rng, 6), axis_at), (blocks,), jnp.float32, low / len(shards), largest / len(shards))
        return jnp.repeat(jnp.exp(draws), shape[axis_at] // blocks).reshape((-1,) + (1,) * (len(shape) - axis_at - 1))

    factor_of = one(*shards[0])
    for cut in shards[1:]:
        factor_of = factor_of * one(*cut)
    return factor_of


def gaussian(stream_key, extent, spread, most, cuts=(), held_as=jnp.bfloat16):
    array = jax.random.normal(stream_key, extent, jnp.float32) * spread
    if len(cuts) > 0:
        array = shard_levels(stream_key, extent, cuts, -0.22, 0.18) * array
    return jnp.clip(array, min=-most, max=most).astype(held_as)


def setup_inputs(seed: int = 0) -> dict:
    seeds = jax.random.split(jax.random.key(seed), 6)
    return {
        "tokens": gaussian(seeds[0], (TOKENS, D), 1.0, 6.0, ((0, 32), (1, 8))),
        "out_grad": gaussian(seeds[1], (TOKENS, D), 1.0, 6.0, ((0, 32), (1, 8))),
        "w_in": gaussian(seeds[2], (D, FF), D ** -0.5, 0.0625, ((0, 8), (1, 32))),
        "w_out": gaussian(seeds[3], (FF, D), FF ** -0.5, 0.046875, ((0, 32), (1, 8))),
        "sketch": gaussian(seeds[4], (TOKENS, SKETCH), SKETCH ** -0.5, 0.375, ((0, 32),)),
    }


inv_root_two = 0.7071067811865476
inv_root_twopi = 0.3989422804014327

def gelu_slope(values):
    return 0.5 * (1.0 + lax.erf(values * inv_root_two)) + values * jnp.exp(-0.5 * values * values) * inv_root_twopi

def reference(tokens, out_grad, w_in, w_out, sketch):
    pre_act = jnp.dot(tokens, w_in, preferred_element_type=jnp.float32)
    hidden = jax.nn.gelu(pre_act, approximate=False).astype(jnp.bfloat16)
    d_hidden = jnp.dot(out_grad, w_out.T, preferred_element_type=jnp.float32)
    d_pre = (d_hidden * gelu_slope(pre_act)).astype(jnp.bfloat16)
    input_grad = jnp.dot(d_pre, w_in.T, preferred_element_type=jnp.float32).astype(jnp.bfloat16)
    sk_tokens = jnp.dot(sketch.T, tokens, preferred_element_type=jnp.float32).astype(jnp.bfloat16)
    sk_grads = jnp.dot(sketch.T, out_grad, preferred_element_type=jnp.float32).astype(jnp.bfloat16)
    sk_hidden = jnp.dot(sketch.T, hidden, preferred_element_type=jnp.float32).astype(jnp.bfloat16)
    sk_dpre = jnp.dot(sketch.T, d_pre, preferred_element_type=jnp.float32).astype(jnp.bfloat16)
    grad_scale = 1.0 / math.sqrt(TOKENS)
    grad_in = (jnp.dot(sk_tokens.T, sk_dpre, preferred_element_type=jnp.float32) * grad_scale).astype(jnp.bfloat16)
    grad_out = (jnp.dot(sk_hidden.T, sk_grads, preferred_element_type=jnp.float32) * grad_scale).astype(jnp.bfloat16)
    return (input_grad, grad_in, grad_out)
```

```python
import math

import jax
import jax.numpy as jnp
from jax import lax
from jax.experimental import pallas as pl
from jax.experimental.pallas import tpu as pltpu
from jax.sharding import PartitionSpec as P

MESH = pl.DeviceIdType.MESH
BF16, F32 = jnp.bfloat16, jnp.float32
inv_root_two = 0.7071067811865476
inv_root_twopi = 0.3989422804014327

ROWS, D, FF, SK = 64, 1024, 512, 256
CHUNKS, SLOTS, CH = 4, 8, 512
BLK = 128
WA = D + SK


def dot(a, b):
    return jnp.dot(a, b, preferred_element_type=F32)


class Copies:
    def __init__(self, send, recv):
        self.send, self.recv, self.count, self.started = send, recv, 0, []

    def start(self, src, dst, device):
        i = self.count
        self.count += 1
        copy = pltpu.make_async_remote_copy(
            src_ref=src,
            dst_ref=dst,
            send_sem=self.send.at[i],
            recv_sem=self.recv.at[i],
            device_id=device,
            device_id_type=MESH,
        )
        copy.start()
        self.started.append(copy)
        return copy


N_COPIES = 148
N_LOCAL = 8


def kernel(
    tok_hbm, grd_hbm, win_hbm, wout_hbm, sk_hbm,
    out_hbm, gin_hbm, gout_hbm,
    GA, GB, WI, WO, WIT, WOT, PA, PB, RA, RB, SAF, SBF, SA, SB, ZA, ZB,
    H, DP, DS, DR, OWN, FX, FR, FS, FZ, ACC, SKT, TOKS, GRDS, HS, DPS, SH, OUT, GI, GO,
    send, recv, lsem,
):
    s, t = lax.axis_index("seq"), lax.axis_index("tp")
    c, x, zl = lax.rem(s, 2), lax.rem(s // 2, 4), s // 8
    y, zh = lax.rem(t, 4), t // 4

    def at(zl_, x_, c_):
        return ((zl_ * 4 + x_) * 2 + c_, t)

    def xdev(d):
        return at(zl, lax.rem(x + d, 4), c)

    zpart = [zl, zl + 1 - 2 * lax.rem(zl, 2), lax.rem(zl + 2, 4), 3 - zl]

    def zdev(k):
        return at(zpart[k], x, c)

    def ydev(d):
        return (s, zh * 4 + lax.rem(y + d, 4))

    sib = at(zl, x, 1 - c)
    zhdev = (s, (1 - zh) * 4 + y)

    def slot(c_, d):
        return c_ * 4 + lax.rem(x + d, 4)

    def block(d):
        return pl.ds(pl.multiple_of(lax.rem(y + d, 4) * BLK, BLK), BLK)

    def cols(n):
        return pl.ds(pl.multiple_of(n * 256, 256), 256)

    me = slot(c, 0)
    loads = [
        pltpu.make_async_copy(tok_hbm, GA.at[0, me, :, pl.ds(0, D)], lsem.at[0]),
        pltpu.make_async_copy(sk_hbm, GA.at[0, me, :, pl.ds(D, SK)], lsem.at[1]),
        pltpu.make_async_copy(grd_hbm, GB.at[0, me], lsem.at[2]),
        pltpu.make_async_copy(win_hbm, WI, lsem.at[3]),
        pltpu.make_async_copy(wout_hbm, WO, lsem.at[4]),
    ]
    for load in loads:
        load.start()
    barrier = pltpu.get_barrier_semaphore()
    partners = [sib, zhdev]
    for d in (1, 2, 3):
        partners += [xdev(d), ydev(d), zdev(d)]
    for device in partners:
        pl.semaphore_signal(barrier, inc=1, device_id=device, device_id_type=MESH)
    pl.semaphore_wait(barrier, len(partners))

    copies = Copies(send, recv)
    rc = copies.start
    U = range(8)

    def gat(u):
        return (GA if u < 4 else GB), u % 4

    zin = {}

    def zsend(u):
        G, k = gat(u)
        zin[u] = rc(G.at[0, me], G.at[k, me], zdev(k))

    full, half, sibs = {}, {}, {}

    def ga(u):
        G, k = gat(u)
        if k:
            zin[u].wait_recv()
        own = G.at[k, me]
        full[u] = [rc(own, own, xdev(1)), rc(own, own, xdev(3))]
        sibs[u] = [rc(own, own, sib)]

    def gb(u):
        G, k = gat(u)
        half[u] = []
        for i, (frm, to, r0) in enumerate(((3, 1, 0), (1, 3, ROWS // 2))):
            full[u][i].wait_recv()
            got = G.at[k, slot(c, frm)]
            part = G.at[k, slot(c, frm), pl.ds(r0, ROWS // 2)]
            half[u].append(rc(part, part, xdev(to)))
            sibs[u].append(rc(got, got, sib))

    def gc(u):
        G, k = gat(u)
        for copy in half[u]:
            copy.wait_recv()
        got = G.at[k, slot(c, 2)]
        sibs[u].append(rc(got, got, sib))

    def tokens_of(u):
        G, k = gat(u)
        return G[k, :, :, 0:D].reshape(CH, D)

    ysent = {}

    def m1(u):
        G, k = gat(u)
        for copy in sibs[u]:
            copy.wait_recv()
        W, Pt, R = (WI, PA, RA) if u < 4 else (WOT, PB, RB)

        @pl.loop(0, FF // 256)
        def _(n):
            Pt[k, :, cols(n)] = dot(tokens_of(u), W[:, cols(n)]).astype(BF16)

        ysent[u] = [
            rc(Pt.at[k, :, block(d)], R.at[k, d - 1], ydev(d)) for d in (1, 2, 3)
        ]

    zhsent = {}

    def ysum(u):
        k = u % 4
        Pt, R, SF, S, Z = (PA, RA, SAF, SA, ZA) if u < 4 else (PB, RB, SBF, SB, ZB)
        for copy in ysent[u]:
            copy.wait_recv()
        total = Pt[k, :, block(0)].astype(F32)
        for i in range(3):
            total += R[k, i].astype(F32)
        SF[k] = total
        S[k] = total.astype(BF16)
        zhsent[u] = rc(S.at[k], Z.at[k], zhdev)

    esent = {}

    def zfin(u):
        k = u % 4
        zhsent[u].wait_recv()
        if u < 4:
            v = SAF[k] + ZA[k].astype(F32)
            phi = 0.5 * (1.0 + lax.erf(v * inv_root_two))
            H[k] = (v * phi).astype(BF16)
            SAF[k] = phi + v * jnp.exp(-0.5 * v * v) * inv_root_twopi
        else:
            dh = SBF[k] + ZB[k].astype(F32)
            DP[k, :, block(0)] = (dh * SAF[k]).astype(BF16)
            mine = DP.at[k, :, block(0)]
            esent[k] = [rc(mine, mine, ydev(d)) for d in (1, 2, 3)]

    dsent = {}

    def m2(k):
        for copy in esent[k]:
            copy.wait_recv()
        other = pl.ds(pl.multiple_of((1 - c) * 256, 256), 256)
        own = pl.ds(pl.multiple_of(c * 256, 256), 256)

        @pl.loop(0, D // 256)
        def _(n):
            DS[k, :, cols(n)] = dot(DP[k, other, :], WIT[:, cols(n)]).astype(BF16)

        dsent[k] = rc(DS.at[k], DR.at[k], sib)

        @pl.loop(0, D // 256)
        def _(n):
            OWN[k, :, cols(n)] = dot(DP[k, own, :], WIT[:, cols(n)])

    fsent = {}

    def f1(k):
        dsent[k].wait_recv()
        FX[k] = (OWN[k] + DR[k].astype(F32)).astype(BF16).reshape(4, ROWS, D)
        fsent[k] = [
            rc(FX.at[k, lax.rem(x + d, 4)], FR.at[k, d - 1], xdev(d)) for d in (1, 2, 3)
        ]

    zback = {}

    def f2(k):
        for copy in fsent[k]:
            copy.wait_recv()
        total = FX[k, x].astype(F32)
        for i in range(3):
            total += FR[k, i].astype(F32)
        if k == 0:
            ACC[...] = total
        else:
            FS[k - 1] = total.astype(BF16)
            zback[k] = rc(FS.at[k - 1], FZ.at[k - 1], zdev(k))

    def f3():
        total = ACC[...]
        for k in (1, 2, 3):
            zback[k].wait_recv()
            total += FZ[k - 1].astype(F32)
        OUT[...] = total.astype(BF16)

    def sk_first(k):
        SKT[k] = GA[k, :, :, D : D + SK].reshape(CH, SK).T

    def sk_wide(u, T):
        k = u % 4

        @pl.loop(0, D // 256)
        def _(n):
            G, _k = gat(u)
            part = dot(SKT[k], G[k, :, :, cols(n)].reshape(CH, 256))
            T[:, cols(n)] = part if k == 0 else T[:, cols(n)] + part

    def sk_hid(k):
        part = dot(SKT[k], H[k])
        HS[...] = part if k == 0 else HS[...] + part

    def sk_dpre(k):
        part = dot(SKT[k], DP[k])
        DPS[...] = part if k == 0 else DPS[...] + part

    hsent = []

    def share_hid():
        SH[:, block(0)] = HS[...].astype(BF16)
        mine = SH.at[:, block(0)]
        hsent.extend(rc(mine, mine, ydev(d)) for d in (1, 2, 3))

    scale = 1.0 / math.sqrt(CH * CHUNKS)
    stores = []

    def grad_out():
        for copy in hsent:
            copy.wait_recv()
        left = SH[...].astype(F32).T.astype(BF16)
        WO[...] = (dot(left, GRDS[...].astype(BF16)) * scale).astype(BF16)
        stores.append(pltpu.make_async_copy(WO, gout_hbm, lsem.at[5]))
        stores[-1].start()

    def grad_in():
        left = TOKS[...].T.astype(BF16)
        WI[...] = (dot(left, DPS[...].astype(BF16)) * scale).astype(BF16)
        stores.append(pltpu.make_async_copy(WI, gin_hbm, lsem.at[6]))
        stores[-1].start()

    loads[0].wait()
    loads[1].wait()
    for u in (1, 2, 3):
        zsend(u)
    ga(0)
    loads[2].wait()
    for u in (5, 6, 7):
        zsend(u)
    loads[3].wait()
    loads[4].wait()
    WOT[...] = WO[...].T
    WIT[...] = WI[...].T
    for tick in range(15):
        if tick + 1 in U:
            ga(tick + 1)
        if tick in U:
            gb(tick)
        if tick - 1 in U:
            gc(tick - 1)
        if tick - 2 in U:
            ysum(tick - 2)
        if tick - 1 in U:
            m1(tick - 1)
        if tick - 4 in U:
            zfin(tick - 4)
        if tick - 9 in range(4):
            m2(tick - 9)
        if tick - 10 in range(4):
            f1(tick - 10)
        if tick - 11 in range(4):
            f2(tick - 11)
        if 2 <= tick < 6:
            sk_first(tick - 2)
            sk_wide(tick - 2, TOKS)
        if 5 <= tick < 9:
            sk_hid(tick - 5)
        if tick == 8:
            share_hid()
        if 7 <= tick < 11:
            sk_wide(tick - 3, GRDS)
        if tick == 11:
            grad_out()
        if 9 <= tick < 13:
            sk_dpre(tick - 9)
        if tick == 13:
            grad_in()
    f3()
    stores.append(pltpu.make_async_copy(OUT, out_hbm, lsem.at[7]))
    stores[-1].start()
    for copy in copies.started:
        copy.wait_send()
    for store in stores:
        store.wait()
    assert copies.count <= N_COPIES


def local(tokens, out_grad, w_in, w_out, sketch):
    def vm(*shape, dtype=BF16):
        return pltpu.VMEM(shape, dtype)

    c4 = CHUNKS
    scratch = [
        vm(c4, SLOTS, ROWS, WA), vm(c4, SLOTS, ROWS, D),
        vm(D, FF), vm(FF, D), vm(FF, D), vm(D, FF),
        vm(c4, CH, FF), vm(c4, CH, FF),
        vm(c4, 3, CH, BLK), vm(c4, 3, CH, BLK),
        vm(c4, CH, BLK, dtype=F32), vm(c4, CH, BLK, dtype=F32),
        vm(c4, CH, BLK), vm(c4, CH, BLK), vm(c4, CH, BLK), vm(c4, CH, BLK),
        vm(c4, CH, BLK), vm(c4, CH, FF),
        vm(c4, 256, D), vm(c4, 256, D), vm(c4, 256, D, dtype=F32),
        vm(c4, 4, ROWS, D), vm(c4, 3, ROWS, D),
        vm(3, ROWS, D), vm(3, ROWS, D), vm(ROWS, D, dtype=F32),
        vm(c4, SK, CH),
        vm(SK, D, dtype=F32), vm(SK, D, dtype=F32),
        vm(SK, BLK, dtype=F32), vm(SK, FF, dtype=F32), vm(SK, FF),
        vm(ROWS, D), vm(8, 128), vm(8, 128),
        pltpu.SemaphoreType.DMA((N_COPIES,)),
        pltpu.SemaphoreType.DMA((N_COPIES,)),
        pltpu.SemaphoreType.DMA((N_LOCAL,)),
    ]
    return pl.pallas_call(
        kernel,
        out_shape=(
            jax.ShapeDtypeStruct((ROWS, D), BF16),
            jax.ShapeDtypeStruct((D, FF), BF16),
            jax.ShapeDtypeStruct((FF, D), BF16),
        ),
        in_specs=[pl.BlockSpec(memory_space=pl.ANY)] * 5,
        out_specs=[pl.BlockSpec(memory_space=pl.ANY)] * 3,
        scratch_shapes=scratch,
        compiler_params=pltpu.CompilerParams(
            collective_id=0, has_side_effects=True, vmem_limit_bytes=60 << 20
        ),
        cost_estimate=pl.CostEstimate(
            flops=10 * 10**9, bytes_accessed=6 * 2**20, transcendentals=2**19
        ),
        name="ffn_grads",
    )(tokens, out_grad, w_in, w_out, sketch)


def solution(mesh):
    return jax.shard_map(
        local,
        mesh=mesh,
        in_specs=(P("seq", "tp"), P("seq", "tp"), P("tp", "seq"), P("seq", "tp"), P("seq", None)),
        out_specs=(P("seq", "tp"), P("tp", "seq"), P("seq", "tp")),
        check_vma=False,
    )
```

```python
import math

import jax
import jax.numpy as jnp
from jax import lax
from jax.experimental import pallas as pl
from jax.experimental.pallas import tpu as pltpu
from jax.sharding import PartitionSpec as P

MESH = pl.DeviceIdType.MESH
BF16, F32 = jnp.bfloat16, jnp.float32
inv_root_two = 0.7071067811865476
inv_root_twopi = 0.3989422804014327

ROWS, D, FF, SK = 64, 1024, 512, 256
CHUNKS, SLOTS, CH = 4, 8, 512
BLK = 128
WA = D + SK
LO, HI = pl.ds(0, CH // 2), pl.ds(CH // 2, CH // 2)
TOP, BOT = pl.ds(0, ROWS // 2), pl.ds(ROWS // 2, ROWS // 2)


def dot(a, b):
    return jnp.dot(a, b, preferred_element_type=F32)


class Copies:
    def __init__(self, send, recv):
        self.send, self.recv, self.count, self.started = send, recv, 0, []

    def start(self, src, dst, device):
        i = self.count
        self.count += 1
        copy = pltpu.make_async_remote_copy(
            src_ref=src,
            dst_ref=dst,
            send_sem=self.send.at[i],
            recv_sem=self.recv.at[i],
            device_id=device,
            device_id_type=MESH,
        )
        copy.start()
        self.started.append(copy)
        return copy


N_COPIES = 200
N_LOCAL = 8

SCHEDULE = (
    ("start", 0), ("ga", 0), ("ga", 4), ("weights", 0), ("gb", 0), ("ga", 1), ("gb", 4),
    ("ga", 5), ("gc", 0), ("m1", 0), ("skf", 0), ("gb", 1), ("skt", 0), ("gc", 4), ("ga", 2),
    ("ymid", 0), ("m1", 4), ("gb", 5), ("skg", 0), ("gc", 1), ("ysum", 0), ("ga", 6), ("ymid", 4),
    ("m1", 1), ("gb", 2), ("gc", 5), ("skf", 1), ("ysum", 4), ("m1", 5), ("gb", 6), ("ymid", 1),
    ("gc", 2), ("ga", 3), ("skg", 1), ("skt", 1), ("ymid", 5), ("gc", 6), ("m1", 2), ("m1", 6),
    ("ysum", 1), ("gb", 3), ("ysum", 5), ("skf", 2), ("ymid", 2), ("zfin", 0), ("ga", 7),
    ("gc", 3), ("ymid", 6), ("zfin", 4), ("m1", 3), ("ysum", 2), ("zfin", 1), ("gb", 7),
    ("ysum", 6), ("skf", 3), ("zfin", 5), ("ymid", 3), ("gc", 7), ("skg", 2), ("skh", 0),
    ("ey", 0), ("m1", 7), ("skg", 3), ("skh", 1), ("zfin", 2), ("ysum", 3), ("efwd", 0),
    ("skh", 2), ("skt", 2), ("ymid", 7), ("zfin", 6), ("skt", 3), ("ey", 1), ("m2", 0),
    ("ysum", 7), ("skd", 0), ("zfin", 3), ("f1", 0), ("efwd", 1), ("skh", 3), ("hz", 3),
    ("ey", 2), ("zfin", 7), ("fmid", 0), ("m2", 1), ("efwd", 2), ("skd", 1), ("hy", 3), ("f1", 1),
    ("f2", 0), ("ey", 3), ("m2", 2), ("fmid", 1), ("skd", 2), ("f1", 2), ("efwd", 3), ("go", 3),
    ("f2", 1), ("fmid", 2), ("m2", 3), ("skd", 3), ("gi", 3), ("f1", 3), ("f2", 2), ("fmid", 3),
    ("f2", 3),
)


def kernel(
    tok_hbm, grd_hbm, win_hbm, wout_hbm, sk_hbm,
    out_hbm, gin_hbm, gout_hbm,
    GA, GB, WI, WO, WIT, WOT, PA, PB, RA, RB, SAF, SBF, SA, SB, ZA, ZB,
    H, DP, DS, DR, OWN, FX, FR, FS, FZ, ACC, SKT, TOKS, GRDS, HS, HB, HZ, DPS, SH, OUT,
    send, recv, lsem,
):
    s, t = lax.axis_index("seq"), lax.axis_index("tp")
    c, x, zl = lax.rem(s, 2), lax.rem(s // 2, 4), s // 8
    y, zh = lax.rem(t, 4), t // 4

    def at(zl_, x_, c_):
        return ((zl_ * 4 + x_) * 2 + c_, t)

    def xdev(d):
        return at(zl, lax.rem(x + d, 4), c)

    zpart = [zl, zl + 1 - 2 * lax.rem(zl, 2), lax.rem(zl + 2, 4), 3 - zl]

    def zdev(k):
        return at(zpart[k], x, c)

    def ydev(d):
        return (s, zh * 4 + lax.rem(y + d, 4))

    sib = at(zl, x, 1 - c)
    zhdev = (s, (1 - zh) * 4 + y)

    def slot(c_, d):
        return c_ * 4 + lax.rem(x + d, 4)

    def xrow(d):
        return lax.rem(x + d, 4)

    def block(d):
        return pl.ds(pl.multiple_of(lax.rem(y + d, 4) * BLK, BLK), BLK)

    def cols(n):
        return pl.ds(pl.multiple_of(n * 256, 256), 256)

    me = slot(c, 0)
    loads = [
        pltpu.make_async_copy(tok_hbm, GA.at[0, me, :, pl.ds(0, D)], lsem.at[0]),
        pltpu.make_async_copy(sk_hbm, GA.at[0, me, :, pl.ds(D, SK)], lsem.at[1]),
        pltpu.make_async_copy(grd_hbm, GB.at[0, me], lsem.at[2]),
        pltpu.make_async_copy(win_hbm, WI, lsem.at[3]),
        pltpu.make_async_copy(wout_hbm, WO, lsem.at[4]),
    ]
    for load in loads:
        load.start()
    barrier = pltpu.get_barrier_semaphore()
    partners = [sib, zhdev]
    for d in (1, 2, 3):
        partners += [xdev(d), ydev(d), zdev(d)]
    for device in partners:
        pl.semaphore_signal(barrier, inc=1, device_id=device, device_id_type=MESH)
    pl.semaphore_wait(barrier, len(partners))

    copies = Copies(send, recv)
    rc = copies.start
    U = range(8)

    def gat(u):
        return (GA if u < 4 else GB), u % 4

    zin = {}

    def zsend(u):
        G, k = gat(u)
        zin[u] = rc(G.at[0, me], G.at[k, me], zdev(k))

    full, half, sibs = {}, {}, {}

    def ga(u):
        G, k = gat(u)
        if k:
            zin[u].wait_recv()
        own = G.at[k, me]
        full[u] = [rc(own, own, xdev(1)), rc(own, own, xdev(3))]
        sibs[u] = [rc(own, own, sib)]

    def gb(u):
        G, k = gat(u)
        half[u] = []
        for i, (frm, to, r0) in enumerate(((3, 1, 0), (1, 3, ROWS // 2))):
            full[u][i].wait_recv()
            got = G.at[k, slot(c, frm)]
            part = G.at[k, slot(c, frm), pl.ds(r0, ROWS // 2)]
            half[u].append(rc(part, part, xdev(to)))
            sibs[u].append(rc(got, got, sib))

    def gc(u):
        G, k = gat(u)
        for copy in half[u]:
            copy.wait_recv()
        got = G.at[k, slot(c, 2)]
        sibs[u].append(rc(got, got, sib))

    def tokens_of(u):
        G, k = gat(u)
        return G[k, :, :, 0:D].reshape(CH, D)

    ysent = {}

    def m1(u):
        G, k = gat(u)
        for copy in sibs[u]:
            copy.wait_recv()
        W, Pt, R = (WI, PA, RA) if u < 4 else (WOT, PB, RB)

        @pl.loop(0, FF // 256)
        def _(n):
            Pt[k, :, cols(n)] = dot(tokens_of(u), W[:, cols(n)]).astype(BF16)

        two, up, down = Pt.at[k, :, block(2)], ydev(1), ydev(3)
        ysent[u] = [
            rc(two.at[LO], R.at[k, 2, LO], up),
            rc(two.at[HI], R.at[k, 2, HI], down),
            rc(Pt.at[k, HI, block(1)], R.at[k, 0, HI], up),
            rc(Pt.at[k, LO, block(3)], R.at[k, 1, LO], down),
        ]

    def ymid(u):
        k = u % 4
        Pt, R = (PA, RA) if u < 4 else (PB, RB)
        for i, (d, half_, to) in enumerate(((1, LO, 0), (3, HI, 1))):
            ysent[u][i].wait_recv()
            Pt[k, half_, block(d)] = (
                Pt[k, half_, block(d)].astype(F32) + R[k, 2, half_].astype(F32)
            ).astype(BF16)
            ysent[u].append(rc(Pt.at[k, half_, block(d)], R.at[k, to, half_], ydev(d)))

    zhsent = {}
    mine_z = pl.ds(pl.multiple_of(zh * (CH // 2), CH // 2), CH // 2)
    theirs_z = pl.ds(pl.multiple_of((1 - zh) * (CH // 2), CH // 2), CH // 2)

    def ysum(u):
        k = u % 4
        Pt, R, SF, S, Z = (PA, RA, SAF, SA, ZA) if u < 4 else (PB, RB, SBF, SB, ZB)
        for copy in ysent[u][2:]:
            copy.wait_recv()

        def total(rows):
            own = Pt[k, rows, block(0)].astype(F32)
            return own + R[k, 0, rows].astype(F32) + R[k, 1, rows].astype(F32)

        S[k] = total(theirs_z).astype(BF16)
        zhsent[u] = rc(S.at[k], Z.at[k], zhdev)
        SF[k] = total(mine_z)

    esent, ezsent = {}, {}

    def zfin(u):
        k = u % 4
        zhsent[u].wait_recv()
        if u < 4:
            v = SAF[k] + ZA[k].astype(F32)
            phi = 0.5 * (1.0 + lax.erf(v * inv_root_two))
            H[k] = (v * phi).astype(BF16)
            SAF[k] = phi + v * jnp.exp(-0.5 * v * v) * inv_root_twopi
        else:
            dh = SBF[k] + ZB[k].astype(F32)
            DP[k, mine_z, block(0)] = (dh * SAF[k]).astype(BF16)
            mine = DP.at[k, mine_z, block(0)]
            ezsent[k] = rc(mine, mine, zhdev)
            esent[k] = [rc(mine, mine, ydev(d)) for d in (1, 3)]

    def ey(k):
        ezsent[k].wait_recv()
        theirs = DP.at[k, theirs_z, block(0)]
        esent[k] += [rc(theirs, theirs, ydev(d)) for d in (1, 3)]

    def efwd(k):
        for i, (frm, to, half_) in enumerate(((3, 1, LO), (1, 3, HI))):
            esent[k][i].wait_recv()
            esent[k][2 + i].wait_recv()
            part = DP.at[k, half_, block(frm)]
            esent[k].append(rc(part, part, ydev(to)))

    dsent = {}

    def m2(k):
        for copy in esent[k][4:]:
            copy.wait_recv()
        other = pl.ds(pl.multiple_of((1 - c) * 256, 256), 256)
        own = pl.ds(pl.multiple_of(c * 256, 256), 256)

        @pl.loop(0, D // 256)
        def _(n):
            DS[k, :, cols(n)] = dot(DP[k, other, :], WIT[:, cols(n)]).astype(BF16)

        dsent[k] = rc(DS.at[k], DR.at[k], sib)

        @pl.loop(0, D // 256)
        def _(n):
            OWN[k, :, cols(n)] = dot(DP[k, own, :], WIT[:, cols(n)])

    fsent = {}

    def f1(k):
        dsent[k].wait_recv()
        FX[k] = (OWN[k] + DR[k].astype(F32)).astype(BF16).reshape(4, ROWS, D)
        two, up, down = xrow(2), xdev(1), xdev(3)
        fsent[k] = [
            rc(FX.at[k, two, TOP], FR.at[k, 2, TOP], up),
            rc(FX.at[k, two, BOT], FR.at[k, 2, BOT], down),
            rc(FX.at[k, xrow(1), BOT], FR.at[k, 0, BOT], up),
            rc(FX.at[k, xrow(3), TOP], FR.at[k, 1, TOP], down),
        ]

    def fmid(k):
        for i, (d, half_, to) in enumerate(((1, TOP, 0), (3, BOT, 1))):
            fsent[k][i].wait_recv()
            FX[k, xrow(d), half_] = (
                FX[k, xrow(d), half_].astype(F32) + FR[k, 2, half_].astype(F32)
            ).astype(BF16)
            fsent[k].append(rc(FX.at[k, xrow(d), half_], FR.at[k, to, half_], xdev(d)))

    zback = {}

    def f2(k):
        for copy in fsent[k][2:]:
            copy.wait_recv()
        total = FX[k, x].astype(F32)
        for i in range(2):
            total += FR[k, i].astype(F32)
        if k == 0:
            ACC[...] = total
        else:
            FS[k - 1] = total.astype(BF16)
            zback[k] = rc(FS.at[k - 1], FZ.at[k - 1], zdev(k))

    def f3():
        total = ACC[...]
        for k in (1, 2, 3):
            zback[k].wait_recv()
            total += FZ[k - 1].astype(F32)
        OUT[...] = total.astype(BF16)

    def sk_first(k):
        SKT[k] = GA[k, :, :, D : D + SK].reshape(CH, SK).T

    def sk_wide(u, T):
        k = u % 4

        @pl.loop(0, D // 256)
        def _(n):
            G, _k = gat(u)
            part = dot(SKT[k], G[k, :, :, cols(n)].reshape(CH, 256))
            T[:, cols(n)] = part if k == 0 else T[:, cols(n)] + part

    def sk_hid(k):
        part = dot(SKT[k, :, mine_z], H[k])
        HS[...] = part if k == 0 else HS[...] + part

    def sk_dpre(k):
        part = dot(SKT[k], DP[k])
        DPS[...] = part if k == 0 else DPS[...] + part

    hsent = []

    def hid_z(k):
        HB[...] = HS[...].astype(BF16)
        hsent.append(rc(HB, HZ, zhdev))

    def hid_y(k):
        hsent.pop().wait_recv()
        SH[:, block(0)] = (HS[...] + HZ[...].astype(F32)).astype(BF16)
        mine = SH.at[:, block(0)]
        hsent.extend(rc(mine, mine, ydev(d)) for d in (1, 2, 3))

    scale = 1.0 / math.sqrt(CH * CHUNKS)
    stores = []

    def grad_out():
        for copy in hsent:
            copy.wait_recv()
        left = SH[...].astype(F32).T.astype(BF16)
        WO[...] = (dot(left, GRDS[...].astype(BF16)) * scale).astype(BF16)
        stores.append(pltpu.make_async_copy(WO, gout_hbm, lsem.at[5]))
        stores[-1].start()

    def grad_in():
        left = TOKS[...].T.astype(BF16)
        WI[...] = (dot(left, DPS[...].astype(BF16)) * scale).astype(BF16)
        stores.append(pltpu.make_async_copy(WI, gin_hbm, lsem.at[6]))
        stores[-1].start()

    def start(_):
        loads[0].wait()
        loads[1].wait()
        loads[2].wait()
        for u in (1, 5, 2, 6, 3, 7):
            zsend(u)

    def weights(_):
        loads[3].wait()
        loads[4].wait()
        WOT[...] = WO[...].T
        WIT[...] = WI[...].T

    stages = dict(
        start=start, weights=weights, ga=ga, gb=gb, gc=gc, m1=m1, ymid=ymid, ysum=ysum, zfin=zfin,
        ey=ey, efwd=efwd, m2=m2, f1=f1, fmid=fmid, f2=f2, skf=sk_first,
        skt=lambda k: sk_wide(k, TOKS), skg=lambda k: sk_wide(k + 4, GRDS), skh=sk_hid,
        skd=sk_dpre, hz=hid_z, hy=hid_y, go=lambda k: grad_out(), gi=lambda k: grad_in(),
    )
    for name, arg in SCHEDULE:
        stages[name](arg)
    f3()
    stores.append(pltpu.make_async_copy(OUT, out_hbm, lsem.at[7]))
    stores[-1].start()
    for copy in copies.started:
        copy.wait_send()
    for store in stores:
        store.wait()
    assert copies.count <= N_COPIES


def local(tokens, out_grad, w_in, w_out, sketch):
    def vm(*shape, dtype=BF16):
        return pltpu.VMEM(shape, dtype)

    c4 = CHUNKS
    scratch = [
        vm(c4, SLOTS, ROWS, WA), vm(c4, SLOTS, ROWS, D),
        vm(D, FF), vm(FF, D), vm(FF, D), vm(D, FF),
        vm(c4, CH, FF), vm(c4, CH, FF),
        vm(c4, 3, CH, BLK), vm(c4, 3, CH, BLK),
        vm(c4, CH // 2, BLK, dtype=F32), vm(c4, CH // 2, BLK, dtype=F32),
        vm(c4, CH // 2, BLK), vm(c4, CH // 2, BLK),
        vm(c4, CH // 2, BLK), vm(c4, CH // 2, BLK),
        vm(c4, CH // 2, BLK), vm(c4, CH, FF),
        vm(c4, 256, D), vm(c4, 256, D), vm(c4, 256, D, dtype=F32),
        vm(c4, 4, ROWS, D), vm(c4, 3, ROWS, D),
        vm(3, ROWS, D), vm(3, ROWS, D), vm(ROWS, D, dtype=F32),
        vm(c4, SK, CH),
        vm(SK, D, dtype=F32), vm(SK, D, dtype=F32),
        vm(SK, BLK, dtype=F32), vm(SK, BLK), vm(SK, BLK),
        vm(SK, FF, dtype=F32), vm(SK, FF),
        vm(ROWS, D),
        pltpu.SemaphoreType.DMA((N_COPIES,)),
        pltpu.SemaphoreType.DMA((N_COPIES,)),
        pltpu.SemaphoreType.DMA((N_LOCAL,)),
    ]
    return pl.pallas_call(
        kernel,
        out_shape=(
            jax.ShapeDtypeStruct((ROWS, D), BF16),
            jax.ShapeDtypeStruct((D, FF), BF16),
            jax.ShapeDtypeStruct((FF, D), BF16),
        ),
        in_specs=[pl.BlockSpec(memory_space=pl.ANY)] * 5,
        out_specs=[pl.BlockSpec(memory_space=pl.ANY)] * 3,
        scratch_shapes=scratch,
        compiler_params=pltpu.CompilerParams(
            collective_id=0, has_side_effects=True, vmem_limit_bytes=60 << 20
        ),
        cost_estimate=pl.CostEstimate(
            flops=10 * 10**9, bytes_accessed=6 * 2**20, transcendentals=2**19
        ),
        name="ffn_grads",
    )(tokens, out_grad, w_in, w_out, sketch)


def solution(mesh):
    return jax.shard_map(
        local,
        mesh=mesh,
        in_specs=(P("seq", "tp"), P("seq", "tp"), P("tp", "seq"), P("seq", "tp"), P("seq", None)),
        out_specs=(P("seq", "tp"), P("tp", "seq"), P("seq", "tp")),
        check_vma=False,
    )
```

```python
import math

import jax
import jax.numpy as jnp
from jax import lax
from jax.experimental import pallas as pl
from jax.experimental.pallas import tpu as pltpu
from jax.sharding import PartitionSpec as P

MESH = pl.DeviceIdType.MESH
BF16, F32 = jnp.bfloat16, jnp.float32
inv_root_two = 0.7071067811865476
inv_root_twopi = 0.3989422804014327

ROWS, D, FF, SK = 64, 1024, 512, 256
CHUNKS, SLOTS, CH = 4, 8, 512
BLK = 128
WA = D + SK
LO, HI = pl.ds(0, CH // 2), pl.ds(CH // 2, CH // 2)
TOP, BOT = pl.ds(0, ROWS // 2), pl.ds(ROWS // 2, ROWS // 2)


def dot(a, b):
    return jnp.dot(a, b, preferred_element_type=F32)


class Copies:
    def __init__(self, send, recv):
        self.send, self.recv, self.count, self.started = send, recv, 0, []

    def start(self, src, dst, device):
        i = self.count
        self.count += 1
        copy = pltpu.make_async_remote_copy(
            src_ref=src,
            dst_ref=dst,
            send_sem=self.send.at[i],
            recv_sem=self.recv.at[i],
            device_id=device,
            device_id_type=MESH,
        )
        copy.start()
        self.started.append(copy)
        return copy


N_COPIES = 200
N_LOCAL = 8

SCHEDULE = (
    ("start", 0), ("ga", 0), ("ga", 4), ("weights", 0), ("gb", 0), ("ga", 1), ("gb", 4),
    ("ga", 5), ("gc", 0), ("m1", 0), ("skf", 0), ("gb", 1), ("skt", 0), ("gc", 4), ("ga", 2),
    ("ymid", 0), ("m1", 4), ("gb", 5), ("skg", 0), ("gc", 1), ("ysum", 0), ("ga", 6), ("ymid", 4),
    ("m1", 1), ("gb", 2), ("gc", 5), ("skf", 1), ("ysum", 4), ("m1", 5), ("gb", 6), ("ymid", 1),
    ("gc", 2), ("ga", 3), ("skg", 1), ("skt", 1), ("ymid", 5), ("gc", 6), ("m1", 2), ("m1", 6),
    ("ysum", 1), ("gb", 3), ("ysum", 5), ("skf", 2), ("ymid", 2), ("zfin", 0), ("ga", 7),
    ("gc", 3), ("ymid", 6), ("zfin", 4), ("m1", 3), ("ysum", 2), ("zfin", 1), ("gb", 7),
    ("ysum", 6), ("skf", 3), ("zfin", 5), ("ymid", 3), ("gc", 7), ("skg", 2), ("skh", 0),
    ("ey", 0), ("m1", 7), ("skg", 3), ("skh", 1), ("zfin", 2), ("ysum", 3), ("efwd", 0),
    ("skh", 2), ("skt", 2), ("ymid", 7), ("zfin", 6), ("skt", 3), ("ey", 1), ("m2", 0),
    ("ysum", 7), ("skd", 0), ("zfin", 3), ("f1", 0), ("efwd", 1), ("skh", 3), ("hz", 3),
    ("ey", 2), ("zfin", 7), ("fmid", 0), ("m2", 1), ("efwd", 2), ("skd", 1), ("hy", 3), ("f1", 1),
    ("f2", 0), ("ey", 3), ("m2", 2), ("fmid", 1), ("skd", 2), ("f1", 2), ("efwd", 3), ("go", 3),
    ("f2", 1), ("fmid", 2), ("m2", 3), ("skd", 3), ("gi", 3), ("f1", 3), ("f2", 2), ("fmid", 3),
    ("f2", 3),
)


def kernel(
    tok_hbm, grd_hbm, win_hbm, wout_hbm, sk_hbm,
    out_hbm, gin_hbm, gout_hbm,
    GA, GB, WI, WO, WIT, WOT, PA, PB, RA, RB, SAF, SBF, SA, SB, ZA, ZB,
    H, DP, DS, DR, FX, FR, FS, FZ, ACC, SKT, TOKS, GRDS, HS, HB, HZ, DPS, SH, OUT,
    send, recv, lsem,
):
    s, t = lax.axis_index("seq"), lax.axis_index("tp")
    c, x, zl = lax.rem(s, 2), lax.rem(s // 2, 4), s // 8
    y, zh = lax.rem(t, 4), t // 4

    def at(zl_, x_, c_):
        return ((zl_ * 4 + x_) * 2 + c_, t)

    def xdev(d):
        return at(zl, lax.rem(x + d, 4), c)

    zpart = [zl, zl + 1 - 2 * lax.rem(zl, 2), lax.rem(zl + 2, 4), 3 - zl]

    def zdev(k):
        return at(zpart[k], x, c)

    def ydev(d):
        return (s, zh * 4 + lax.rem(y + d, 4))

    sib = at(zl, x, 1 - c)
    zhdev = (s, (1 - zh) * 4 + y)

    def slot(c_, d):
        return c_ * 4 + lax.rem(x + d, 4)

    def xrow(d):
        return lax.rem(x + d, 4)

    def block(d):
        return pl.ds(pl.multiple_of(lax.rem(y + d, 4) * BLK, BLK), BLK)

    def cols(n):
        return pl.ds(pl.multiple_of(n * 256, 256), 256)

    me = slot(c, 0)
    loads = [
        pltpu.make_async_copy(tok_hbm, GA.at[0, me, :, pl.ds(0, D)], lsem.at[0]),
        pltpu.make_async_copy(sk_hbm, GA.at[0, me, :, pl.ds(D, SK)], lsem.at[1]),
        pltpu.make_async_copy(grd_hbm, GB.at[0, me], lsem.at[2]),
        pltpu.make_async_copy(win_hbm, WI, lsem.at[3]),
        pltpu.make_async_copy(wout_hbm, WO, lsem.at[4]),
    ]
    for load in loads:
        load.start()
    barrier = pltpu.get_barrier_semaphore()
    partners = [sib, zhdev]
    for d in (1, 2, 3):
        partners += [xdev(d), ydev(d), zdev(d)]
    for device in partners:
        pl.semaphore_signal(barrier, inc=1, device_id=device, device_id_type=MESH)
    pl.semaphore_wait(barrier, len(partners))

    copies = Copies(send, recv)
    rc = copies.start
    U = range(8)

    def gat(u):
        return (GA if u < 4 else GB), u % 4

    zin = {}

    def zsend(u):
        G, k = gat(u)
        zin[u] = rc(G.at[0, me], G.at[k, me], zdev(k))

    full, half, sibs = {}, {}, {}

    def ga(u):
        G, k = gat(u)
        if k:
            zin[u].wait_recv()
        own = G.at[k, me]
        full[u] = [rc(own, own, xdev(1)), rc(own, own, xdev(3))]
        sibs[u] = [rc(own, own, sib)]

    def gb(u):
        G, k = gat(u)
        half[u] = []
        for i, (frm, to, r0) in enumerate(((3, 1, 0), (1, 3, ROWS // 2))):
            full[u][i].wait_recv()
            got = G.at[k, slot(c, frm)]
            part = G.at[k, slot(c, frm), pl.ds(r0, ROWS // 2)]
            half[u].append(rc(part, part, xdev(to)))
            sibs[u].append(rc(got, got, sib))

    def gc(u):
        G, k = gat(u)
        for copy in half[u]:
            copy.wait_recv()
        got = G.at[k, slot(c, 2)]
        sibs[u].append(rc(got, got, sib))

    def tokens_of(u):
        G, k = gat(u)
        return G[k, :, :, 0:D].reshape(CH, D)

    ysent = {}

    def m1(u):
        G, k = gat(u)
        for copy in sibs[u]:
            copy.wait_recv()
        W, Pt, R = (WI, PA, RA) if u < 4 else (WOT, PB, RB)

        @pl.loop(0, FF // 256)
        def _(n):
            Pt[k, :, cols(n)] = dot(tokens_of(u), W[:, cols(n)]).astype(BF16)

        two, up, down = Pt.at[k, :, block(2)], ydev(1), ydev(3)
        ysent[u] = [
            rc(two.at[LO], R.at[k, 2, LO], up),
            rc(two.at[HI], R.at[k, 2, HI], down),
            rc(Pt.at[k, HI, block(1)], R.at[k, 0, HI], up),
            rc(Pt.at[k, LO, block(3)], R.at[k, 1, LO], down),
        ]

    def ymid(u):
        k = u % 4
        Pt, R = (PA, RA) if u < 4 else (PB, RB)
        for i, (d, half_, to) in enumerate(((1, LO, 0), (3, HI, 1))):
            ysent[u][i].wait_recv()
            Pt[k, half_, block(d)] = (
                Pt[k, half_, block(d)].astype(F32) + R[k, 2, half_].astype(F32)
            ).astype(BF16)
            ysent[u].append(rc(Pt.at[k, half_, block(d)], R.at[k, to, half_], ydev(d)))

    zhsent = {}
    mine_z = pl.ds(pl.multiple_of(zh * (CH // 2), CH // 2), CH // 2)
    theirs_z = pl.ds(pl.multiple_of((1 - zh) * (CH // 2), CH // 2), CH // 2)

    def ysum(u):
        k = u % 4
        Pt, R, SF, S, Z = (PA, RA, SAF, SA, ZA) if u < 4 else (PB, RB, SBF, SB, ZB)
        for copy in ysent[u][2:]:
            copy.wait_recv()

        def total(rows):
            own = Pt[k, rows, block(0)].astype(F32)
            return own + R[k, 0, rows].astype(F32) + R[k, 1, rows].astype(F32)

        S[k] = total(theirs_z).astype(BF16)
        zhsent[u] = rc(S.at[k], Z.at[k], zhdev)
        SF[k] = total(mine_z)

    esent, ezsent = {}, {}

    def zfin(u):
        k = u % 4
        zhsent[u].wait_recv()
        if u < 4:
            v = SAF[k] + ZA[k].astype(F32)
            phi = 0.5 * (1.0 + lax.erf(v * inv_root_two))
            H[k] = (v * phi).astype(BF16)
            SAF[k] = phi + v * jnp.exp(-0.5 * v * v) * inv_root_twopi
        else:
            dh = SBF[k] + ZB[k].astype(F32)
            DP[k, mine_z, block(0)] = (dh * SAF[k]).astype(BF16)
            mine = DP.at[k, mine_z, block(0)]
            ezsent[k] = rc(mine, mine, zhdev)
            esent[k] = [rc(mine, mine, ydev(d)) for d in (1, 3)]

    def ey(k):
        ezsent[k].wait_recv()
        theirs = DP.at[k, theirs_z, block(0)]
        esent[k] += [rc(theirs, theirs, ydev(d)) for d in (1, 3)]

    def efwd(k):
        for i, (frm, to, half_) in enumerate(((3, 1, LO), (1, 3, HI))):
            esent[k][i].wait_recv()
            esent[k][2 + i].wait_recv()
            part = DP.at[k, half_, block(frm)]
            esent[k].append(rc(part, part, ydev(to)))

    dsent = {}
    mine_c = pl.ds(pl.multiple_of(c * (CH // 2), CH // 2), CH // 2)
    theirs_c = pl.ds(pl.multiple_of((1 - c) * (CH // 2), CH // 2), CH // 2)

    def m2(k):
        for copy in esent[k][4:]:
            copy.wait_recv()

        @pl.loop(0, D // 256)
        def _(n):
            DS[k, :, cols(n)] = dot(DP[k], WIT[:, cols(n)]).astype(BF16)

        dsent[k] = rc(DS.at[k, theirs_c], DR.at[k], sib)

    fsent = {}

    def f1(k):
        dsent[k].wait_recv()
        FX[k] = (DS[k, mine_c].astype(F32) + DR[k].astype(F32)).astype(BF16).reshape(4, ROWS, D)
        two, up, down = xrow(2), xdev(1), xdev(3)
        fsent[k] = [
            rc(FX.at[k, two, TOP], FR.at[k, 2, TOP], up),
            rc(FX.at[k, two, BOT], FR.at[k, 2, BOT], down),
            rc(FX.at[k, xrow(1), BOT], FR.at[k, 0, BOT], up),
            rc(FX.at[k, xrow(3), TOP], FR.at[k, 1, TOP], down),
        ]

    def fmid(k):
        for i, (d, half_, to) in enumerate(((1, TOP, 0), (3, BOT, 1))):
            fsent[k][i].wait_recv()
            FX[k, xrow(d), half_] = (
                FX[k, xrow(d), half_].astype(F32) + FR[k, 2, half_].astype(F32)
            ).astype(BF16)
            fsent[k].append(rc(FX.at[k, xrow(d), half_], FR.at[k, to, half_], xdev(d)))

    zback = {}

    def f2(k):
        for copy in fsent[k][2:]:
            copy.wait_recv()
        total = FX[k, x].astype(F32)
        for i in range(2):
            total += FR[k, i].astype(F32)
        if k == 0:
            ACC[...] = total
        else:
            FS[k - 1] = total.astype(BF16)
            zback[k] = rc(FS.at[k - 1], FZ.at[k - 1], zdev(k))

    def f3():
        total = ACC[...]
        for k in (1, 2, 3):
            zback[k].wait_recv()
            total += FZ[k - 1].astype(F32)
        OUT[...] = total.astype(BF16)

    def sk_first(k):
        SKT[k] = GA[k, :, :, D : D + SK].reshape(CH, SK).T

    def sk_wide(u, T):
        k = u % 4

        @pl.loop(0, D // 256)
        def _(n):
            G, _k = gat(u)
            part = dot(SKT[k], G[k, :, :, cols(n)].reshape(CH, 256))
            T[:, cols(n)] = part if k == 0 else T[:, cols(n)] + part

    def sk_hid(k):
        part = dot(SKT[k, :, mine_z], H[k])
        HS[...] = part if k == 0 else HS[...] + part

    def sk_dpre(k):
        part = dot(SKT[k], DP[k])
        DPS[...] = part if k == 0 else DPS[...] + part

    hsent = []

    def hid_z(k):
        HB[...] = HS[...].astype(BF16)
        hsent.append(rc(HB, HZ, zhdev))

    def hid_y(k):
        hsent.pop().wait_recv()
        SH[:, block(0)] = (HS[...] + HZ[...].astype(F32)).astype(BF16)
        mine = SH.at[:, block(0)]
        hsent.extend(rc(mine, mine, ydev(d)) for d in (1, 2, 3))

    scale = 1.0 / math.sqrt(CH * CHUNKS)
    stores = []

    def grad_out():
        for copy in hsent:
            copy.wait_recv()
        left = SH[...].astype(F32).T.astype(BF16)
        WO[...] = (dot(left, GRDS[...].astype(BF16)) * scale).astype(BF16)
        stores.append(pltpu.make_async_copy(WO, gout_hbm, lsem.at[5]))
        stores[-1].start()

    def grad_in():
        left = TOKS[...].T.astype(BF16)
        WI[...] = (dot(left, DPS[...].astype(BF16)) * scale).astype(BF16)
        stores.append(pltpu.make_async_copy(WI, gin_hbm, lsem.at[6]))
        stores[-1].start()

    def start(_):
        loads[0].wait()
        loads[1].wait()
        loads[2].wait()
        for u in (1, 5, 2, 6, 3, 7):
            zsend(u)

    def weights(_):
        loads[3].wait()
        loads[4].wait()
        WOT[...] = WO[...].T
        WIT[...] = WI[...].T

    stages = dict(
        start=start, weights=weights, ga=ga, gb=gb, gc=gc, m1=m1, ymid=ymid, ysum=ysum, zfin=zfin,
        ey=ey, efwd=efwd, m2=m2, f1=f1, fmid=fmid, f2=f2, skf=sk_first,
        skt=lambda k: sk_wide(k, TOKS), skg=lambda k: sk_wide(k + 4, GRDS), skh=sk_hid,
        skd=sk_dpre, hz=hid_z, hy=hid_y, go=lambda k: grad_out(), gi=lambda k: grad_in(),
    )
    for name, arg in SCHEDULE:
        stages[name](arg)
    f3()
    stores.append(pltpu.make_async_copy(OUT, out_hbm, lsem.at[7]))
    stores[-1].start()
    for copy in copies.started:
        copy.wait_send()
    for store in stores:
        store.wait()
    assert copies.count <= N_COPIES


def hand_on(a, b, c, a_out, b_out, c_out, a_buf, b_buf, c_buf, sems):
    parts = [(b, b_buf, b_out, i) for i in range(4)] + [(c, c_buf, c_out, i) for i in range(4)]
    loads, stores = [], []
    for n, (src, buf, dst, i) in enumerate(parts + [(a, a_buf, a_out, None)]):
        if i is not None:
            rows = src.shape[0] // 4
            src, buf, dst = (r.at[pl.ds(i * rows, rows)] for r in (src, buf, dst))
        loads.append(pltpu.make_async_copy(src, buf, sems.at[0, n]))
        stores.append(pltpu.make_async_copy(buf, dst, sems.at[1, n]))
    for load in loads:
        load.start()
    for load, store in zip(loads, stores):
        load.wait()
        store.start()
    for store in stores:
        store.wait()


def local(tokens, out_grad, w_in, w_out, sketch):
    def vm(*shape, dtype=BF16):
        return pltpu.VMEM(shape, dtype)

    c4 = CHUNKS
    scratch = [
        vm(c4, SLOTS, ROWS, WA), vm(c4, SLOTS, ROWS, D),
        vm(D, FF), vm(FF, D), vm(FF, D), vm(D, FF),
        vm(c4, CH, FF), vm(c4, CH, FF),
        vm(c4, 3, CH, BLK), vm(c4, 3, CH, BLK),
        vm(c4, CH // 2, BLK, dtype=F32), vm(c4, CH // 2, BLK, dtype=F32),
        vm(c4, CH // 2, BLK), vm(c4, CH // 2, BLK),
        vm(c4, CH // 2, BLK), vm(c4, CH // 2, BLK),
        vm(c4, CH // 2, BLK), vm(c4, CH, FF),
        vm(c4, CH, D), vm(c4, CH // 2, D),
        vm(c4, 4, ROWS, D), vm(c4, 3, ROWS, D),
        vm(3, ROWS, D), vm(3, ROWS, D), vm(ROWS, D, dtype=F32),
        vm(c4, SK, CH),
        vm(SK, D, dtype=F32), vm(SK, D, dtype=F32),
        vm(SK, BLK, dtype=F32), vm(SK, BLK), vm(SK, BLK),
        vm(SK, FF, dtype=F32), vm(SK, FF),
        vm(ROWS, D),
        pltpu.SemaphoreType.DMA((N_COPIES,)),
        pltpu.SemaphoreType.DMA((N_COPIES,)),
        pltpu.SemaphoreType.DMA((N_LOCAL,)),
    ]
    results = pl.pallas_call(
        kernel,
        out_shape=(
            jax.ShapeDtypeStruct((ROWS, D), BF16),
            jax.ShapeDtypeStruct((D, FF), BF16),
            jax.ShapeDtypeStruct((FF, D), BF16),
        ),
        in_specs=[pl.BlockSpec(memory_space=pl.ANY)] * 5,
        out_specs=[pl.BlockSpec(memory_space=pl.ANY)] * 3,
        scratch_shapes=scratch,
        compiler_params=pltpu.CompilerParams(
            collective_id=0, has_side_effects=True, vmem_limit_bytes=60 << 20
        ),
        cost_estimate=pl.CostEstimate(
            flops=10 * 10**9, bytes_accessed=6 * 2**20, transcendentals=2**19
        ),
        name="ffn_grads",
    )(tokens, out_grad, w_in, w_out, sketch)
    return pl.pallas_call(
        hand_on,
        out_shape=tuple(jax.ShapeDtypeStruct(r.shape, r.dtype) for r in results),
        in_specs=[pl.BlockSpec(memory_space=pl.ANY)] * 3,
        out_specs=[pl.BlockSpec(memory_space=pl.ANY)] * 3,
        scratch_shapes=[vm(*r.shape) for r in results] + [pltpu.SemaphoreType.DMA((2, 9))],
        name="hand_on",
    )(*results)


def solution(mesh):
    return jax.shard_map(
        local,
        mesh=mesh,
        in_specs=(P("seq", "tp"), P("seq", "tp"), P("tp", "seq"), P("seq", "tp"), P("seq", None)),
        out_specs=(P("seq", "tp"), P("tp", "seq"), P("seq", "tp")),
        check_vma=False,
    )
```

```python
import math

import jax
import jax.numpy as jnp
from jax import lax
from jax.experimental import pallas as pl
from jax.experimental.pallas import tpu as pltpu
from jax.sharding import PartitionSpec as P

MESH = pl.DeviceIdType.MESH
BF16, F32 = jnp.bfloat16, jnp.float32
inv_root_two = 0.7071067811865476
inv_root_twopi = 0.3989422804014327

ROWS, D, FF, SK = 64, 1024, 512, 256
CHUNKS, SLOTS, CH = 4, 8, 512
BLK = 128
WA = D + SK
LO, HI = pl.ds(0, CH // 2), pl.ds(CH // 2, CH // 2)
TOP, BOT = pl.ds(0, ROWS // 2), pl.ds(ROWS // 2, ROWS // 2)


def dot(a, b):
    return jnp.dot(a, b, preferred_element_type=F32)


class Copies:
    def __init__(self, send, recv):
        self.send, self.recv, self.count, self.started = send, recv, 0, []

    def start(self, src, dst, device):
        i = self.count
        self.count += 1
        copy = pltpu.make_async_remote_copy(
            src_ref=src,
            dst_ref=dst,
            send_sem=self.send.at[i],
            recv_sem=self.recv.at[i],
            device_id=device,
            device_id_type=MESH,
        )
        copy.start()
        self.started.append(copy)
        return copy


N_COPIES = 220
N_LOCAL = 8

SCHEDULE = (
    ("start", 0), ("ga", 0), ("ga", 4), ("weights", 0), ("gb", 0), ("ga", 1), ("gb", 4),
    ("ga", 5), ("gc", 0), ("m1", 0), ("skf", 0), ("gb", 1), ("skt", 0), ("gc", 4), ("ga", 2),
    ("ymid", 0), ("m1", 4), ("gb", 5), ("skg", 0), ("gc", 1), ("ysum", 0), ("ga", 6), ("ymid", 4),
    ("m1", 1), ("gb", 2), ("gc", 5), ("skf", 1), ("ysum", 4), ("m1", 5), ("gb", 6), ("ymid", 1),
    ("gc", 2), ("ga", 3), ("skg", 1), ("skt", 1), ("ymid", 5), ("gc", 6), ("m1", 2), ("m1", 6),
    ("ysum", 1), ("gb", 3), ("ysum", 5), ("skf", 2), ("ymid", 2), ("zfin", 0), ("ga", 7),
    ("gc", 3), ("ymid", 6), ("zfin", 4), ("m1", 3), ("ysum", 2), ("zfin", 1), ("gb", 7),
    ("ysum", 6), ("skf", 3), ("zfin", 5), ("ymid", 3), ("gc", 7), ("skg", 2), ("skh", 0),
    ("ey", 0), ("m1", 7), ("skg", 3), ("skh", 1), ("zfin", 2), ("ysum", 3), ("efwd", 0),
    ("skh", 2), ("skt", 2), ("ymid", 7), ("zfin", 6), ("skt", 3), ("ey", 1), ("m2", 0),
    ("ysum", 7), ("skd", 0), ("zfin", 3), ("f1", 0), ("efwd", 1), ("skh", 3), ("hz", 3),
    ("ey", 2), ("zfin", 7), ("fmid", 0), ("m2", 1), ("efwd", 2), ("skd", 1), ("hy", 3), ("f1", 1),
    ("f2", 0), ("ey", 3), ("m2", 2), ("fmid", 1), ("skd", 2), ("f1", 2), ("efwd", 3), ("go", 3),
    ("f2", 1), ("fmid", 2), ("m2", 3), ("skd", 3), ("gi", 3), ("f1", 3), ("f2", 2), ("fmid", 3),
    ("f2", 3),
)


def kernel(
    tok_hbm, grd_hbm, win_hbm, wout_hbm, sk_hbm,
    out_hbm, gin_hbm, gout_hbm,
    GA, GB, WI, WO, WIT, WOT, PA, PB, RA, RB, SAF, SBF, SA, SB, ZA, ZB,
    H, DP, DS, DR, FX, FR, FS, FZ, ACC, SKT, TOKS, GRDS, HS, HB, HZ, DPS, SH, OUT,
    send, recv, lsem,
):
    s, t = lax.axis_index("seq"), lax.axis_index("tp")
    c, x, zl = lax.rem(s, 2), lax.rem(s // 2, 4), s // 8
    y, zh = lax.rem(t, 4), t // 4

    def at(zl_, x_, c_):
        return ((zl_ * 4 + x_) * 2 + c_, t)

    def xdev(d):
        return at(zl, lax.rem(x + d, 4), c)

    zpart = [zl, zl + 1 - 2 * lax.rem(zl, 2), lax.rem(zl + 2, 4), 3 - zl]

    def zdev(k):
        return at(zpart[k], x, c)

    def ydev(d):
        return (s, zh * 4 + lax.rem(y + d, 4))

    sib = at(zl, x, 1 - c)
    zhdev = (s, (1 - zh) * 4 + y)

    def slot(c_, d):
        return c_ * 4 + lax.rem(x + d, 4)

    def xrow(d):
        return lax.rem(x + d, 4)

    def block(d):
        return pl.ds(pl.multiple_of(lax.rem(y + d, 4) * BLK, BLK), BLK)

    def cols(n):
        return pl.ds(pl.multiple_of(n * 256, 256), 256)

    me = slot(c, 0)
    loads = [
        pltpu.make_async_copy(tok_hbm, GA.at[0, me, :, pl.ds(0, D)], lsem.at[0]),
        pltpu.make_async_copy(sk_hbm, GA.at[0, me, :, pl.ds(D, SK)], lsem.at[1]),
        pltpu.make_async_copy(grd_hbm, GB.at[0, me], lsem.at[2]),
        pltpu.make_async_copy(win_hbm, WI, lsem.at[3]),
        pltpu.make_async_copy(wout_hbm, WO, lsem.at[4]),
    ]
    for load in loads:
        load.start()
    barrier = pltpu.get_barrier_semaphore()
    partners = [sib, zhdev]
    for d in (1, 2, 3):
        partners += [xdev(d), ydev(d), zdev(d)]
    for device in partners:
        pl.semaphore_signal(barrier, inc=1, device_id=device, device_id_type=MESH)
    pl.semaphore_wait(barrier, len(partners))

    copies = Copies(send, recv)
    rc = copies.start
    U = range(8)

    def gat(u):
        return (GA if u < 4 else GB), u % 4

    zin = {}

    def zsend(u):
        G, k = gat(u)
        zin[u] = rc(G.at[0, me], G.at[k, me], zdev(k))

    full, half, sibs = {}, {}, {}

    def ga(u):
        G, k = gat(u)
        if k:
            zin[u].wait_recv()
        own = G.at[k, me]
        top, bottom = G.at[k, me, TOP], G.at[k, me, BOT]
        full[u] = [
            rc(top, top, xdev(1)),
            rc(bottom, bottom, xdev(3)),
            rc(bottom, bottom, xdev(1)),
            rc(top, top, xdev(3)),
        ]
        sibs[u] = [rc(own, own, sib)]

    def gb(u):
        G, k = gat(u)
        half[u] = []
        for i, (frm, to, r0) in enumerate(((3, 1, 0), (1, 3, ROWS // 2))):
            full[u][i].wait_recv()
            part = G.at[k, slot(c, frm), pl.ds(r0, ROWS // 2)]
            half[u].append(rc(part, part, xdev(to)))
        for i, frm in enumerate((3, 1)):
            full[u][2 + i].wait_recv()
            got = G.at[k, slot(c, frm)]
            sibs[u].append(rc(got, got, sib))

    def gc(u):
        G, k = gat(u)
        for copy in half[u]:
            copy.wait_recv()
        got = G.at[k, slot(c, 2)]
        sibs[u].append(rc(got, got, sib))

    def tokens_of(u):
        G, k = gat(u)
        return G[k, :, :, 0:D].reshape(CH, D)

    ysent = {}

    def m1(u):
        G, k = gat(u)
        for copy in sibs[u]:
            copy.wait_recv()
        W, Pt, R = (WI, PA, RA) if u < 4 else (WOT, PB, RB)

        def columns(n):
            Pt[k, :, cols(n)] = dot(tokens_of(u), W[:, cols(n)]).astype(BF16)

        two, up, down = Pt.at[k, :, block(2)], ydev(1), ydev(3)
        first = lax.rem(y + 2, 4) // 2
        columns(first)
        ysent[u] = [
            rc(two.at[LO], R.at[k, 2, LO], up),
            rc(two.at[HI], R.at[k, 2, HI], down),
        ]
        columns(1 - first)
        ysent[u] += [
            rc(Pt.at[k, HI, block(1)], R.at[k, 0, HI], up),
            rc(Pt.at[k, LO, block(3)], R.at[k, 1, LO], down),
        ]

    def ymid(u):
        k = u % 4
        Pt, R = (PA, RA) if u < 4 else (PB, RB)
        for i, (d, half_, to) in enumerate(((1, LO, 0), (3, HI, 1))):
            ysent[u][i].wait_recv()
            Pt[k, half_, block(d)] = (
                Pt[k, half_, block(d)].astype(F32) + R[k, 2, half_].astype(F32)
            ).astype(BF16)
            ysent[u].append(rc(Pt.at[k, half_, block(d)], R.at[k, to, half_], ydev(d)))

    zhsent = {}
    mine_z = pl.ds(pl.multiple_of(zh * (CH // 2), CH // 2), CH // 2)
    theirs_z = pl.ds(pl.multiple_of((1 - zh) * (CH // 2), CH // 2), CH // 2)

    def ysum(u):
        k = u % 4
        Pt, R, SF, S, Z = (PA, RA, SAF, SA, ZA) if u < 4 else (PB, RB, SBF, SB, ZB)
        for copy in ysent[u][2:]:
            copy.wait_recv()

        def total(rows):
            own = Pt[k, rows, block(0)].astype(F32)
            return own + R[k, 0, rows].astype(F32) + R[k, 1, rows].astype(F32)

        S[k] = total(theirs_z).astype(BF16)
        zhsent[u] = rc(S.at[k], Z.at[k], zhdev)
        SF[k] = total(mine_z)

    esent, ezsent = {}, {}

    def zfin(u):
        k = u % 4
        zhsent[u].wait_recv()
        if u < 4:
            v = SAF[k] + ZA[k].astype(F32)
            phi = 0.5 * (1.0 + lax.erf(v * inv_root_two))
            H[k] = (v * phi).astype(BF16)
            SAF[k] = phi + v * jnp.exp(-0.5 * v * v) * inv_root_twopi
        else:
            dh = SBF[k] + ZB[k].astype(F32)
            DP[k, mine_z, block(0)] = (dh * SAF[k]).astype(BF16)
            mine = DP.at[k, mine_z, block(0)]
            ezsent[k] = rc(mine, mine, zhdev)
            esent[k] = [rc(mine, mine, ydev(d)) for d in (1, 3)]

    def ey(k):
        ezsent[k].wait_recv()
        theirs = DP.at[k, theirs_z, block(0)]
        esent[k] += [rc(theirs, theirs, ydev(d)) for d in (1, 3)]

    def efwd(k):
        for i, (frm, to, half_) in enumerate(((3, 1, LO), (1, 3, HI))):
            esent[k][i].wait_recv()
            esent[k][2 + i].wait_recv()
            part = DP.at[k, half_, block(frm)]
            esent[k].append(rc(part, part, ydev(to)))

    dsent = {}
    mine_c = pl.ds(pl.multiple_of(c * (CH // 2), CH // 2), CH // 2)
    theirs_c = pl.ds(pl.multiple_of((1 - c) * (CH // 2), CH // 2), CH // 2)

    def m2(k):
        for copy in esent[k][4:]:
            copy.wait_recv()

        @pl.loop(0, D // 256)
        def _(n):
            DS[k, :, cols(n)] = dot(DP[k], WIT[:, cols(n)]).astype(BF16)

        dsent[k] = rc(DS.at[k, theirs_c], DR.at[k], sib)

    fsent = {}

    def f1(k):
        dsent[k].wait_recv()
        FX[k] = (DS[k, mine_c].astype(F32) + DR[k].astype(F32)).astype(BF16).reshape(4, ROWS, D)
        two, up, down = xrow(2), xdev(1), xdev(3)
        fsent[k] = [
            rc(FX.at[k, two, TOP], FR.at[k, 2, TOP], up),
            rc(FX.at[k, two, BOT], FR.at[k, 2, BOT], down),
            rc(FX.at[k, xrow(1), BOT], FR.at[k, 0, BOT], up),
            rc(FX.at[k, xrow(3), TOP], FR.at[k, 1, TOP], down),
        ]

    def fmid(k):
        for i, (d, half_, to) in enumerate(((1, TOP, 0), (3, BOT, 1))):
            fsent[k][i].wait_recv()
            FX[k, xrow(d), half_] = (
                FX[k, xrow(d), half_].astype(F32) + FR[k, 2, half_].astype(F32)
            ).astype(BF16)
            fsent[k].append(rc(FX.at[k, xrow(d), half_], FR.at[k, to, half_], xdev(d)))

    zback = {}

    def f2(k):
        for copy in fsent[k][2:]:
            copy.wait_recv()
        total = FX[k, x].astype(F32)
        for i in range(2):
            total += FR[k, i].astype(F32)
        if k == 0:
            ACC[...] = total
        else:
            FS[k - 1] = total.astype(BF16)
            zback[k] = rc(FS.at[k - 1], FZ.at[k - 1], zdev(k))

    def f3():
        total = ACC[...]
        for k in (1, 2, 3):
            zback[k].wait_recv()
            total += FZ[k - 1].astype(F32)
        OUT[...] = total.astype(BF16)

    def sk_first(k):
        SKT[k] = GA[k, :, :, D : D + SK].reshape(CH, SK).T

    def sk_wide(u, T):
        k = u % 4

        @pl.loop(0, D // 256)
        def _(n):
            G, _k = gat(u)
            part = dot(SKT[k], G[k, :, :, cols(n)].reshape(CH, 256))
            T[:, cols(n)] = part if k == 0 else T[:, cols(n)] + part

    def sk_hid(k):
        part = dot(SKT[k, :, mine_z], H[k])
        HS[...] = part if k == 0 else HS[...] + part

    def sk_dpre(k):
        part = dot(SKT[k], DP[k])
        DPS[...] = part if k == 0 else DPS[...] + part

    hsent = []

    def hid_z(k):
        HB[...] = HS[...].astype(BF16)
        hsent.append(rc(HB, HZ, zhdev))

    def hid_y(k):
        hsent.pop().wait_recv()
        SH[:, block(0)] = (HS[...] + HZ[...].astype(F32)).astype(BF16)
        mine = SH.at[:, block(0)]
        hsent.extend(rc(mine, mine, ydev(d)) for d in (1, 2, 3))

    scale = 1.0 / math.sqrt(CH * CHUNKS)
    stores = []

    def grad_out():
        for copy in hsent:
            copy.wait_recv()
        left = SH[...].astype(F32).T.astype(BF16)
        WO[...] = (dot(left, GRDS[...].astype(BF16)) * scale).astype(BF16)
        stores.append(pltpu.make_async_copy(WO, gout_hbm, lsem.at[5]))
        stores[-1].start()

    def grad_in():
        left = TOKS[...].T.astype(BF16)
        WI[...] = (dot(left, DPS[...].astype(BF16)) * scale).astype(BF16)
        stores.append(pltpu.make_async_copy(WI, gin_hbm, lsem.at[6]))
        stores[-1].start()

    def start(_):
        loads[0].wait()
        loads[1].wait()
        loads[2].wait()
        for u in (1, 5, 2, 6, 3, 7):
            zsend(u)

    def weights(_):
        loads[3].wait()
        loads[4].wait()
        WOT[...] = WO[...].T
        WIT[...] = WI[...].T

    stages = dict(
        start=start, weights=weights, ga=ga, gb=gb, gc=gc, m1=m1, ymid=ymid, ysum=ysum, zfin=zfin,
        ey=ey, efwd=efwd, m2=m2, f1=f1, fmid=fmid, f2=f2, skf=sk_first,
        skt=lambda k: sk_wide(k, TOKS), skg=lambda k: sk_wide(k + 4, GRDS), skh=sk_hid,
        skd=sk_dpre, hz=hid_z, hy=hid_y, go=lambda k: grad_out(), gi=lambda k: grad_in(),
    )
    for name, arg in SCHEDULE:
        stages[name](arg)
    f3()
    stores.append(pltpu.make_async_copy(OUT, out_hbm, lsem.at[7]))
    stores[-1].start()
    for copy in copies.started:
        copy.wait_send()
    for store in stores:
        store.wait()
    assert copies.count <= N_COPIES


def hand_on(a, b, c, a_out, b_out, c_out, a_buf, b_buf, c_buf, sems):
    parts = [(b, b_buf, b_out, i) for i in range(4)] + [(c, c_buf, c_out, i) for i in range(4)]
    loads, stores = [], []
    for n, (src, buf, dst, i) in enumerate(parts + [(a, a_buf, a_out, None)]):
        if i is not None:
            rows = src.shape[0] // 4
            src, buf, dst = (r.at[pl.ds(i * rows, rows)] for r in (src, buf, dst))
        loads.append(pltpu.make_async_copy(src, buf, sems.at[0, n]))
        stores.append(pltpu.make_async_copy(buf, dst, sems.at[1, n]))
    for load in loads:
        load.start()
    for load, store in zip(loads, stores):
        load.wait()
        store.start()
    for store in stores:
        store.wait()


def local(tokens, out_grad, w_in, w_out, sketch):
    def vm(*shape, dtype=BF16):
        return pltpu.VMEM(shape, dtype)

    c4 = CHUNKS
    scratch = [
        vm(c4, SLOTS, ROWS, WA), vm(c4, SLOTS, ROWS, D),
        vm(D, FF), vm(FF, D), vm(FF, D), vm(D, FF),
        vm(c4, CH, FF), vm(c4, CH, FF),
        vm(c4, 3, CH, BLK), vm(c4, 3, CH, BLK),
        vm(c4, CH // 2, BLK, dtype=F32), vm(c4, CH // 2, BLK, dtype=F32),
        vm(c4, CH // 2, BLK), vm(c4, CH // 2, BLK),
        vm(c4, CH // 2, BLK), vm(c4, CH // 2, BLK),
        vm(c4, CH // 2, BLK), vm(c4, CH, FF),
        vm(c4, CH, D), vm(c4, CH // 2, D),
        vm(c4, 4, ROWS, D), vm(c4, 3, ROWS, D),
        vm(3, ROWS, D), vm(3, ROWS, D), vm(ROWS, D, dtype=F32),
        vm(c4, SK, CH),
        vm(SK, D, dtype=F32), vm(SK, D, dtype=F32),
        vm(SK, BLK, dtype=F32), vm(SK, BLK), vm(SK, BLK),
        vm(SK, FF, dtype=F32), vm(SK, FF),
        vm(ROWS, D),
        pltpu.SemaphoreType.DMA((N_COPIES,)),
        pltpu.SemaphoreType.DMA((N_COPIES,)),
        pltpu.SemaphoreType.DMA((N_LOCAL,)),
    ]
    results = pl.pallas_call(
        kernel,
        out_shape=(
            jax.ShapeDtypeStruct((ROWS, D), BF16),
            jax.ShapeDtypeStruct((D, FF), BF16),
            jax.ShapeDtypeStruct((FF, D), BF16),
        ),
        in_specs=[pl.BlockSpec(memory_space=pl.ANY)] * 5,
        out_specs=[pl.BlockSpec(memory_space=pl.ANY)] * 3,
        scratch_shapes=scratch,
        compiler_params=pltpu.CompilerParams(
            collective_id=0, has_side_effects=True, vmem_limit_bytes=60 << 20
        ),
        cost_estimate=pl.CostEstimate(
            flops=10 * 10**9, bytes_accessed=6 * 2**20, transcendentals=2**19
        ),
        name="ffn_grads",
    )(tokens, out_grad, w_in, w_out, sketch)
    return pl.pallas_call(
        hand_on,
        out_shape=tuple(jax.ShapeDtypeStruct(r.shape, r.dtype) for r in results),
        in_specs=[pl.BlockSpec(memory_space=pl.ANY)] * 3,
        out_specs=[pl.BlockSpec(memory_space=pl.ANY)] * 3,
        scratch_shapes=[vm(*r.shape) for r in results] + [pltpu.SemaphoreType.DMA((2, 9))],
        name="hand_on",
    )(*results)


def solution(mesh):
    return jax.shard_map(
        local,
        mesh=mesh,
        in_specs=(P("seq", "tp"), P("seq", "tp"), P("tp", "seq"), P("seq", "tp"), P("seq", None)),
        out_specs=(P("seq", "tp"), P("tp", "seq"), P("seq", "tp")),
        check_vma=False,
    )
```
